32 devices in a mesh: vol: 16 (over z, y, core), sub: 2 (over x).
Axes of the slice: x: 2, y: 2, z: 4, core: 2. Of those that a mesh axis runs over, the one named last changes fastest.
Arguments:
- load: float32 [3, 20, 24576], P(None, None, ('vol', 'sub'))
- stiffness: float32 [24576], P(('vol', 'sub')), may hold values from 0.5 to 4
- material: int32 [24576], P(('vol', 'sub')), may hold values from 0 to 1
- stiffness_ref: float32 [2, 60, 60], replicated, as said below
- face_trace: float32 [4, 10, 20], replicated
- adjacency: int32 [4, 24576], P(None, ('vol', 'sub')), may hold values from -1 to 4095, as said below
- penalty: float32 [4, 24576], P(None, ('vol', 'sub')), as said below
- halo_sub: int32 [16384], P(('vol', 'sub')), may hold values from -1 to 3071, as said below
- halo_vol: int32 [16384], P(('vol', 'sub')), may hold values from 0 to 3071, as said below
- fault_send: int32 [4096], P(('vol', 'sub')), may hold values from -1 to 3071, as said below
- fault_target: int32 [4096], P(('vol', 'sub')), may hold values from -1 to 127, as said below
- fault_angles: float32 [2, 4096], P(None, ('vol', 'sub')), may hold values from -3.140625 to 3.140625
- slip_rate: float32 [10, 4096], P(None, ('vol', 'sub')), may hold values from 0.001 to 1
- sigma_eff: float32 [10, 4096], P(None, ('vol', 'sub')), may hold values from 1 to 4
Outputs:
- solution: float32 [3, 20, 24576], P(None, None, ('vol', 'sub'))
- residual: float32 [3, 20, 24576], P(None, None, ('vol', 'sub'))
- slip_next: float32 [10, 4096], P(None, ('vol', 'sub'))
- sigma_next: float32 [10, 4096], P(None, ('vol', 'sub'))
The draws below stay inside these ranges and needn't reach their ends.
Inputs may be any that keep to these rules, and one draw needn't show every extreme that they name: `adjacency`: A face end paired inside its partition gets the partner's code f * 768 + e; a shared one gets 4 * 768 plus its position among the received columns; -1 is a domain boundary. Pairing is symmetric. `penalty`: paired face ends carry equal weights. `halo_sub`: local face-end codes, distinct within a partition; the block for the partition itself is all -1. `halo_vol`: local face-end codes, distinct within a partition and from those of halo_sub. `fault_send`: each block of 64 slots holds its live codes first, then -1; some partition fills every block in each vol row. Every live code's partner lies in the same partition. `fault_target`: live exactly where fault_send is; the live targets of one grid cell are distinct. `stiffness_ref`: symmetric and diagonally dominant with positive diagonal.
All inputs are finite; a program needn't handle non-finite values.
Results may differ from the reference program's by a relative error of at most 0.0065.
Values sent between devices are 32-bit elements; how exact they have to be, the bound alone decides.
A program may use at most 64 MiB of HBM per device.

```python
import math
import jax
import jax.numpy as jnp
from jax import lax

E_DEV = 768
HS = 256
HV = 256
NBND = 256
FAULT_DEV = 128
ITERS = 2
NODES = 20
FACE_NODES = 10
NELEM = 24576
NFAULT = 4096
FCAP = 64
N_VOL = 16
N_SUB = 2


def layout(key):
    devices = N_VOL * N_SUB
    ends = 4 * E_DEV
    keys = jax.random.split(jax.random.fold_in(key, 101), devices)
    orders = jax.vmap(lambda one_key: jax.random.permutation(one_key, ends))(keys).astype(jnp.int32)
    inverse = jnp.argsort(orders, axis=1, stable=True).astype(jnp.int32)
    return (orders, inverse)


def partner_position():
    ends = 4 * E_DEV
    base = N_SUB * HS + 2 * HV + NBND
    position = jnp.arange(ends, dtype=jnp.int32)
    paired = base + jnp.bitwise_xor(position - base, 1)
    return (position, jnp.where(position >= base, paired, position))


def self_blocks(position):
    devices = N_VOL * N_SUB
    sub_home = (jnp.arange(devices, dtype=jnp.int32) % N_SUB)[:, None]
    return (position[None, :] < N_SUB * HS) & (position[None, :] // HS == sub_home)


def to_global(by_code):
    devices = N_VOL * N_SUB
    return by_code.reshape(devices, 4, E_DEV).transpose(1, 0, 2).reshape(4, devices * E_DEV)


def fault_plan(key):
    orders, inverse = layout(key)
    devices = N_VOL * N_SUB
    base = N_SUB * HS + 2 * HV + NBND
    cap = FAULT_DEV // N_SUB
    plan_key = jax.random.fold_in(key, 202)
    hot_sender = jax.random.randint(jax.random.fold_in(plan_key, 1), (N_VOL, 1, 1), 0, N_SUB)
    other_counts = jax.random.randint(jax.random.fold_in(plan_key, 2), (N_VOL, N_SUB, N_SUB), 0, cap // 2 + 1)
    sender = jnp.arange(N_SUB, dtype=jnp.int32)[None, :, None]
    counts = jnp.where(sender == hot_sender, cap, other_counts)
    live = jnp.arange(cap, dtype=jnp.int32)[None, None, None, :] < counts[:, :, :, None]
    dest_keys = jax.random.split(jax.random.fold_in(plan_key, 3), devices)
    dest_orders = jax.vmap(lambda one_key: jax.random.permutation(one_key, FAULT_DEV))(dest_keys).astype(jnp.int32)
    targets = dest_orders.reshape(N_VOL, N_SUB, N_SUB, cap).transpose(0, 2, 1, 3)
    targets = jnp.where(live, targets, -1).reshape(devices * FAULT_DEV)
    codes = orders[:, base:base + FAULT_DEV].reshape(N_VOL, N_SUB, N_SUB, cap)
    codes = jnp.where(live, codes, -1).reshape(devices * FAULT_DEV)
    return (codes, targets)


def draw_adjacency(key, part):
    orders, inverse = layout(key)
    ends = 4 * E_DEV
    remote = N_SUB * HS + 2 * HV
    base = remote + NBND
    position, partner = partner_position()
    local_code = jnp.take_along_axis(orders, jnp.broadcast_to(partner[None, :], orders.shape), axis=1)
    shared = jnp.where(position[None, :] < remote, ends + position[None, :], -1)
    by_position = jnp.where(position[None, :] >= base, local_code, shared)
    by_position = jnp.where(self_blocks(position), -1, by_position)
    return to_global(jnp.take_along_axis(by_position, inverse, axis=1))


def draw_halo_sub(key, part):
    orders, inverse = layout(key)
    position, partner = partner_position()
    sub_len = N_SUB * HS
    blocks = jnp.where(self_blocks(position)[:, :sub_len], -1, orders[:, :sub_len])
    return blocks.reshape(-1)


def draw_halo_vol(key, part):
    orders, inverse = layout(key)
    sub_len = N_SUB * HS
    return orders[:, sub_len:sub_len + 2 * HV].reshape(-1)


def draw_fault_send(key, part):
    codes, targets = fault_plan(key)
    return codes


def draw_fault_target(key, part):
    codes, targets = fault_plan(key)
    return targets


def draw_penalty(key, part):
    orders, inverse = layout(key)
    key = jax.random.fold_in(key, 6)
    devices = N_VOL * N_SUB
    ends = 4 * E_DEV
    sub_len = N_SUB * HS
    remote = sub_len + 2 * HV
    base = remote + NBND
    weights = jnp.exp(jax.random.uniform(key, (devices, ends), dtype=jnp.float32, minval=0.0, maxval=1.3862944))
    position, partner = partner_position()
    local_mean = 0.5 * (weights + jnp.take_along_axis(weights, jnp.broadcast_to(partner[None, :], weights.shape), axis=1))
    sub_part = weights[:, :sub_len].reshape(N_VOL, N_SUB, N_SUB, HS)
    sub_mean = (0.5 * (sub_part + sub_part.transpose(0, 2, 1, 3))).reshape(devices, sub_len)
    vols = weights[:, sub_len:remote].reshape(N_VOL, N_SUB, 2, HV)
    down, upward = (vols[:, :, 0, :], vols[:, :, 1, :])
    up_prev = jnp.concatenate([down[:1], upward[:-1]], axis=0)
    down_next = jnp.concatenate([down[1:], upward[-1:]], axis=0)
    vol_mean = jnp.stack([0.5 * (down + up_prev), 0.5 * (upward + down_next)], axis=2).reshape(devices, 2 * HV)
    by_position = jnp.concatenate([sub_mean, vol_mean, weights[:, remote:base], local_mean[:, base:]], axis=1)
    return to_global(jnp.take_along_axis(by_position, inverse, axis=1))


def draw_stiffness_ref(key, part):
    key = jax.random.fold_in(key, 7)
    order = 3 * NODES
    raw = jax.random.uniform(jax.random.fold_in(key, 1), (2, order, order), dtype=jnp.float32, minval=-1.0, maxval=1.0)
    identity = jnp.eye(order, dtype=jnp.float32)
    off_part = 0.5 * (raw + jnp.swapaxes(raw, 1, 2)) * (1.0 - identity)
    spread = jax.random.uniform(jax.random.fold_in(key, 2), (2, order), dtype=jnp.float32)
    leading = float(order) + 30.0 * spread
    return (off_part + leading[:, :, None] * identity) / float(order)


def draw_face_trace(key, part):
    key = jax.random.fold_in(key, 9)
    noise = jax.random.normal(key, (4, FACE_NODES, NODES), dtype=jnp.float32)
    return (1.0 + noise) * (0.5 / float(NODES)) ** 0.5


def draw_load(key, part):
    key = jax.random.fold_in(key, 8)
    elem_index = jnp.arange(NELEM, dtype=jnp.int32)
    rising = 1.0 + 2.0 * elem_index.astype(jnp.float32) / float(NELEM)
    column = elem_index // E_DEV % N_SUB
    smooth_side = 2 * column >= N_SUB
    rough = jax.random.normal(jax.random.fold_in(key, 1), (3, NODES, NELEM), dtype=jnp.float32)
    common = jax.random.normal(jax.random.fold_in(key, 2), (3, 1, NELEM), dtype=jnp.float32)
    values = jnp.where(smooth_side[None, None, :], common + 0.3 * rough, rough)
    return values * rising[None, None, :]


def with_ends(drawn, stream_key, least, top_value):
    place = [jax.random.randint(jax.random.fold_in(stream_key, axis), (), 0, length) for axis, length in enumerate(drawn.shape)]
    longest = drawn.shape.index(max(drawn.shape))
    next_to = place[:longest] + [(place[longest] + 1) % drawn.shape[longest]] + place[longest + 1:]
    return drawn.at[tuple(place)].set(least).at[tuple(next_to)].set(top_value)


def block_scale(rng, extent, cuts, smallest, high):
    loudness, own = 1.0, jax.random.fold_in(rng, 6)
    for dim, parts in cuts:
        steps = jnp.exp(jax.random.uniform(jax.random.fold_in(own, dim), (parts,), jnp.float32, smallest / len(cuts), high / len(cuts)))
        loudness = loudness * jnp.repeat(steps, extent[dim] // parts).reshape([-1 if axis == dim else 1 for axis in range(len(extent))])
    return loudness


def setup_inputs(seed: int = 0) -> dict:
    key_of = jax.random.split(jax.random.key(seed), 15)
    return {
        "load": draw_load(jax.random.fold_in(key_of[14], 71), 0),
        "stiffness": jnp.clip(jnp.exp(math.log(4.0) - 2.0794415 * jax.random.uniform(key_of[1], (NELEM,), jnp.float32) ** block_scale(key_of[1], (NELEM,), ((0, 32),), -0.2, 0.2)), 0.5, 4.0),
        "material": with_ends(jax.random.randint(key_of[2], (NELEM,), 0, 2), jax.random.fold_in(key_of[2], 1), 0, 1).astype(jnp.int32),
        "stiffness_ref": draw_stiffness_ref(jax.random.fold_in(key_of[14], 71), 0),
        "face_trace": draw_face_trace(jax.random.fold_in(key_of[14], 71), 0),
        "adjacency": draw_adjacency(jax.random.fold_in(key_of[14], 71), 0),
        "penalty": draw_penalty(jax.random.fold_in(key_of[14], 71), 0),
        "halo_sub": draw_halo_sub(jax.random.fold_in(key_of[14], 71), 0),
        "halo_vol": draw_halo_vol(jax.random.fold_in(key_of[14], 71), 0),
        "fault_send": draw_fault_send(jax.random.fold_in(key_of[14], 71), 0),
        "fault_target": draw_fault_target(jax.random.fold_in(key_of[14], 71), 0),
        "fault_angles": jnp.clip(jax.random.uniform(key_of[11], (2, NFAULT), jnp.float32, -3.140625, 3.140625), -3.140625, 3.140625),
        "slip_rate": jnp.clip(jnp.exp(math.log(1.0) - 6.9077552 * jax.random.uniform(key_of[12], (FACE_NODES, NFAULT), jnp.float32) ** block_scale(key_of[12], (FACE_NODES, NFAULT), ((1, 32),), -0.2, 0.2)), 0.001, 1.0),
        "sigma_eff": jnp.clip(1.0 + 3.0 * jax.random.uniform(key_of[13], (FACE_NODES, NFAULT), jnp.float32) ** block_scale(key_of[13], (FACE_NODES, NFAULT), ((1, 32),), -0.2, 0.2), 1.0, 4.0),
    }


HIGHEST = lax.Precision.HIGHEST
FRICTION = 0.4
SIGMA_BACK = 3.0
RATE_LENGTH = 0.5
SPEED_REF = 0.2
RATE_DAMP = 0.5
SHEAR_SOFT = 0.01

def face_values(nodal_field, face_trace):
    comps, nodes, elems = nodal_field.shape
    faces, face_nodes = (face_trace.shape[0], face_trace.shape[1])
    traced = jnp.einsum('fij,cje->cife', face_trace, nodal_field, precision=HIGHEST)
    return traced.reshape(comps * face_nodes, faces * elems)

def pick_columns(source, codes):
    taken = jnp.take(source, jnp.maximum(codes, 0), axis=1)
    return jnp.where(codes[None, :] >= 0, taken, jnp.zeros_like(taken))

def penalty_flux(traces, remote_cols, adjacency, penalty):
    extended = jnp.concatenate([traces, remote_cols], axis=1)
    nearby = pick_columns(extended, adjacency)
    return penalty[None, :] * (traces - nearby)

def apply_local(nodal_field, traces, remote_cols, adjacency, penalty, stiffness, material, stiffness_ref, face_trace):
    comps, nodes, elems = nodal_field.shape
    faces, face_nodes = (face_trace.shape[0], face_trace.shape[1])
    flux_term = penalty_flux(traces, remote_cols, adjacency, penalty).reshape(comps, face_nodes, faces, elems)
    face_part = jnp.einsum('fij,cife->cje', face_trace, flux_term, precision=HIGHEST)
    flat_field = nodal_field.reshape(comps * nodes, elems)
    both_kinds = jnp.einsum('mab,be->mae', stiffness_ref, flat_field, precision=HIGHEST)
    volume_part = jnp.where(material[None, :] == 1, both_kinds[1], both_kinds[0]) * stiffness[None, :]
    return volume_part.reshape(comps, nodes, elems) + face_part

def jacobi_diag(penalty, stiffness, material, stiffness_ref, face_trace):
    faces, face_nodes, nodes = face_trace.shape
    elems = stiffness.shape[0]
    ref_diag = jnp.diagonal(stiffness_ref, axis1=1, axis2=2)
    volume_part = jnp.where(material[None, :] == 1, ref_diag[1][:, None], ref_diag[0][:, None]) * stiffness[None, :]
    face_part = jnp.einsum('fij,fe->je', face_trace * face_trace, penalty.reshape(faces, elems), precision=HIGHEST)
    comps = ref_diag.shape[1] // nodes
    return volume_part.reshape(comps, nodes, elems) + face_part[None, :, :]

def friction_update(traction, fault_angles, slip_rate, sigma_eff):
    face_nodes = slip_rate.shape[0]
    vectors = traction.reshape(3, face_nodes, -1)
    polar, azimuth = (fault_angles[0], fault_angles[1])
    normal = jnp.stack([jnp.sin(polar) * jnp.cos(azimuth), jnp.sin(polar) * jnp.sin(azimuth), jnp.cos(polar)])
    normal_part = lax.optimization_barrier(jnp.sum(vectors * normal[:, None, :], axis=0))
    shear_vec = vectors - normal_part[None, :, :] * normal[:, None, :]
    shear_size = jnp.sqrt(lax.optimization_barrier(jnp.sum(shear_vec * shear_vec, axis=0)) + SHEAR_SOFT)
    normal_stress = SIGMA_BACK - normal_part
    sigma_new = sigma_eff - RATE_LENGTH * (slip_rate + SPEED_REF) * (sigma_eff - normal_stress)
    slip_new = jnp.maximum(slip_rate + RATE_DAMP * (shear_size - FRICTION * sigma_new), 0.0)
    return (slip_new, sigma_new)

def reference(load, stiffness, material, stiffness_ref, face_trace, adjacency, penalty, halo_sub, halo_vol, fault_send, fault_target, fault_angles, slip_rate, sigma_eff):
    devices = N_VOL * N_SUB
    ends = 4 * E_DEV
    rows = 3 * FACE_NODES
    load_dev = load.reshape(3, NODES, devices, E_DEV).transpose(2, 0, 1, 3)
    stiff_dev = stiffness.reshape(devices, E_DEV)
    mat_dev = material.reshape(devices, E_DEV)
    adj_dev = adjacency.reshape(4, devices, E_DEV).transpose(1, 0, 2).reshape(devices, ends)
    pen_dev = penalty.reshape(4, devices, E_DEV).transpose(1, 0, 2).reshape(devices, ends)
    sub_dev = halo_sub.reshape(devices, N_SUB * HS)
    vol_dev = halo_vol.reshape(devices, 2 * HV)
    send_dev = fault_send.reshape(devices, FAULT_DEV)

    def remote_all(fields):

        def sends(items):
            field_one, sub_one, vol_one = items
            traces = face_values(field_one, face_trace)
            return (pick_columns(traces, sub_one), pick_columns(traces, vol_one))
        sub_send, vol_send = lax.map(sends, (fields, sub_dev, vol_dev))
        received = sub_send.reshape(N_VOL, N_SUB, rows, N_SUB, HS).transpose(0, 3, 2, 1, 4).reshape(devices, rows, N_SUB * HS)
        vols = vol_send.reshape(N_VOL, N_SUB, rows, 2 * HV)
        empty = jnp.zeros_like(vols[:1, :, :, :HV])
        lower = jnp.concatenate([empty, vols[:-1, :, :, HV:]], axis=0)
        upper = jnp.concatenate([vols[1:, :, :, :HV], empty], axis=0)
        return jnp.concatenate([received, lower.reshape(devices, rows, HV), upper.reshape(devices, rows, HV)], axis=2)

    def operator(fields):
        remote_cols = remote_all(fields)

        def single(items):
            field_one, remote_one, adj_one, pen_one, stiff_one, mat_one = items
            traces = face_values(field_one, face_trace)
            return apply_local(field_one, traces, remote_one, adj_one, pen_one, stiff_one, mat_one, stiffness_ref, face_trace)
        return lax.map(single, (fields, remote_cols, adj_dev, pen_dev, stiff_dev, mat_dev))
    precond = jax.vmap(lambda pen_one, stiff_one, mat_one: jacobi_diag(pen_one, stiff_one, mat_one, stiffness_ref, face_trace))(pen_dev, stiff_dev, mat_dev)
    solution = jnp.zeros_like(load_dev)
    residual = load_dev
    scaled = residual / precond
    search = scaled
    resid_dot = jnp.sum(residual * scaled)
    for sweep_idx in range(ITERS):
        image_vec = operator(search)
        step_len = resid_dot / jnp.sum(search * image_vec)
        solution = solution + step_len * search
        residual = residual - step_len * image_vec
        if sweep_idx + 1 < ITERS:
            scaled = residual / precond
            resid_new = jnp.sum(residual * scaled)
            search = scaled + resid_new / resid_dot * search
            resid_dot = resid_new
    remote_cols = remote_all(solution)

    def fault_flux(items):
        field_one, remote_one, adj_one, pen_one, codes_one = items
        traces = face_values(field_one, face_trace)
        return pick_columns(penalty_flux(traces, remote_one, adj_one, pen_one), codes_one)
    sent = lax.map(fault_flux, (solution, remote_cols, adj_dev, pen_dev, send_dev))
    received = sent.reshape(N_VOL, N_SUB, rows, N_SUB, FCAP).transpose(0, 3, 2, 1, 4).reshape(devices, rows, FAULT_DEV)
    targets = fault_target.reshape(N_VOL, N_SUB, N_SUB, FCAP).transpose(0, 2, 1, 3).reshape(devices, FAULT_DEV)
    onehot = (targets[:, :, None] == jnp.arange(FAULT_DEV, dtype=jnp.int32)[None, None, :]).astype(jnp.float32)
    traction_dev = jnp.einsum('drk,dks->drs', received, onehot, precision=HIGHEST)
    traction = traction_dev.transpose(1, 0, 2).reshape(rows, devices * FAULT_DEV)
    slip_new, sigma_new = friction_update(traction, fault_angles, slip_rate, sigma_eff)
    solution_out = solution.transpose(1, 2, 0, 3).reshape(3, NODES, NELEM)
    residual_out = residual.transpose(1, 2, 0, 3).reshape(3, NODES, NELEM)
    return (solution_out, residual_out, slip_new, sigma_new)
```

```python
import functools

import jax
import jax.numpy as jnp
from jax import lax
from jax.experimental import pallas as pl
from jax.experimental.pallas import tpu as pltpu
from jax.sharding import PartitionSpec as P

FRICTION = 0.4
SIGMA_BACK = 3.0
RATE_LENGTH = 0.5
SPEED_REF = 0.2
RATE_DAMP = 0.5
SHEAR_SOFT = 0.01

HIGHEST = lax.Precision.HIGHEST
MESH = pl.DeviceIdType.MESH
F32, BF16 = jnp.float32, jnp.bfloat16
LANES = 128
ROWS = 32
STRIDE = 24
FIELD = 80


def iota(shape, dim):
    return lax.broadcasted_iota(jnp.int32, shape, dim)


def exact_dot(a, b):
    return lax.dot(a, b, precision=HIGHEST, preferred_element_type=F32)


def split(x):
    high = x.astype(BF16)
    return high, (x - high.astype(F32)).astype(BF16)


def fold_rows(x):
    total = x[0:8]
    for i in range(8, x.shape[0], 8):
        total = total + x[i : i + 8]
    return total


def pick(codes, sources, first, start):
    group = jnp.broadcast_to(lax.shift_right_arithmetic(codes, 7), (8, LANES))
    lane = jnp.broadcast_to(jnp.bitwise_and(codes, LANES - 1), (8, LANES))
    out = [start[8 * r : 8 * r + 8] for r in range(ROWS // 8)]
    for i, source in enumerate(sources):
        hit = group == first + i
        block = source()
        for r in range(ROWS // 8):
            taken = jnp.take_along_axis(
                block[8 * r : 8 * r + 8], lane, axis=1, mode="promise_in_bounds"
            )
            out[r] = jnp.where(hit, taken, out[r])
    return jnp.concatenate(out, axis=0)


def kernel(
    sizes,
    load,
    stiff,
    material,
    stiffness_ref,
    face_trace,
    adjacency,
    penalty,
    halo_sub,
    halo_vol,
    fault_send,
    fault_target,
    angles,
    slip,
    sigma,
    solution_out,
    residual_out,
    slip_out,
    sigma_out,
    field,
    field3,
    ops,
    back3,
    diag_inv,
    trace,
    near,
    flux,
    volume,
    image,
    send_buf,
    recv_buf,
    fault_codes,
    fault_buf,
    fault_recv,
    sums,
    sums_two,
    grid,
    halo_s,
    halo_r,
    fault_s,
    fault_r,
    sum_s,
    sum_r,
):
    n_vol, n_sub, gs, gv, tiles, flat = sizes
    elems = tiles * LANES
    v, s = lax.axis_index("vol"), lax.axis_index("sub")
    n_groups = 4 * tiles
    n_remote = n_sub * gs + 2 * gv

    def sub_peer(d):
        return (v, lax.rem(s + d, n_sub))

    def vol_peer(d):
        return (lax.rem(v + d, n_vol), s)

    def any_peer(d):
        place = lax.rem(v * n_sub + s + d, n_vol * n_sub)
        return (lax.div(place, n_sub), lax.rem(place, n_sub))

    recv_buf[...] = jnp.zeros_like(recv_buf)
    barrier = pltpu.get_barrier_semaphore()
    rounds = [(any_peer, n_vol * n_sub)] if flat else [(sub_peer, n_sub), (vol_peer, n_vol)]
    for peer, count in rounds:

        def greet(d, carry, peer=peer):
            pl.semaphore_signal(barrier, inc=1, device_id=peer(d), device_id_type=MESH)
            return carry

        lax.fori_loop(1, count, greet, 0)

    wide = 256
    col = iota((20, wide), 1)
    inner = lax.rem(col, FIELD)
    node_of = jnp.where((col < 3 * FIELD) & (inner < 3 * STRIDE), lax.rem(inner, STRIDE), -1)
    spread = (node_of == iota((20, wide), 0)).astype(F32)
    row = iota((ROWS, 10), 0)
    lift = ((lax.rem(row, 10) == iota((ROWS, 10), 1)) & (row < 30)).astype(F32)
    same = lax.div(iota((ROWS, wide), 0), 10) == lax.div(
        lax.rem(iota((ROWS, wide), 1), FIELD), STRIDE
    )
    third = iota((1, wide), 1) >= 2 * FIELD

    def store_op(at, value):
        high, low = split(value)
        ops[pl.ds(at, value.shape[0]), :] = jnp.where(
            third, low.astype(F32), high.astype(F32)
        ).astype(BF16)

    faces = []
    for f in range(4):
        full = exact_dot(exact_dot(lift, face_trace[f]), spread)
        faces.append(jnp.where(same, full, 0.0))
    face_all = jnp.concatenate(faces, axis=0)
    store_op(0, face_all)
    back = jnp.transpose(face_all[:, :LANES])[:FIELD]
    back_high, back_low = split(back)
    back3[...] = jnp.concatenate([back_high, back_high, back_low], axis=1)

    a60 = iota((60, wide), 0)
    c60 = iota((60, wide), 1)
    in60 = lax.rem(c60, FIELD)
    place60 = lax.div(in60, STRIDE) * 20 + lax.rem(in60, STRIDE)
    ok60 = (c60 < 3 * FIELD) & (in60 < 3 * STRIDE) & (lax.rem(in60, STRIDE) < 20)
    right = (ok60 & (place60 == a60)).astype(F32)
    rows60 = iota((FIELD, 60), 0)
    left = (
        (rows60 < 3 * STRIDE)
        & (lax.rem(rows60, STRIDE) < 20)
        & (lax.div(rows60, STRIDE) * 20 + lax.rem(rows60, STRIDE) == iota((FIELD, 60), 1))
    ).astype(F32)
    eye = iota((FIELD, wide), 0) == iota((FIELD, wide), 1)
    pad_row = iota((FIELD, 1), 0)
    is_pad = (pad_row >= 3 * STRIDE) | (lax.rem(pad_row, STRIDE) >= 20)
    diag = []
    for m in range(2):
        ref = exact_dot(exact_dot(left, stiffness_ref[m]), right)
        store_op(LANES + m * FIELD, ref)
        entries = jnp.sum(jnp.where(eye, ref, 0.0), axis=1, keepdims=True)
        diag.append(jnp.where(is_pad, 1.0, entries))
    squares = back * back
    weights = []
    lane_face = lax.div(iota((FIELD, LANES), 1), ROWS)
    for f in range(4):
        weights.append(jnp.sum(jnp.where(lane_face == f, squares, 0.0), axis=1, keepdims=True))

    field[...] = jnp.zeros_like(field)
    for c in range(3):
        field[1, c * STRIDE : c * STRIDE + 20, :] = load[c]
    material_one = material[...] == 1
    precond = jnp.where(material_one, diag[1], diag[0]) * stiff[...]
    for f in range(4):
        precond = precond + weights[f] * penalty[f : f + 1, :]
    diag_inv[...] = 1.0 / precond
    field[0] = field[1] * diag_inv[...]

    def make_traces(index, phase):
        high, low = split(field[index])
        field3[...] = jnp.concatenate(
            [high, low, high, jnp.zeros((wide - 3 * FIELD, elems), BF16)], axis=0
        )
        for k in range(tiles):
            trace[phase, k] = lax.dot(
                ops[:LANES, :],
                field3[:, k * LANES : (k + 1) * LANES],
                preferred_element_type=F32,
            )

    def local_sources(ref, phase):
        def source(g):
            return lambda: ref[phase, g % tiles, (g // tiles) * ROWS : (g // tiles + 1) * ROWS, :]

        return [source(g) for g in range(n_groups)]

    nothing = jnp.zeros((ROWS, LANES), F32)

    def halo_copy(phase, i, src, dst, count, device):
        return pltpu.make_async_remote_copy(
            src_ref=send_buf.at[phase, pl.ds(src, count)],
            dst_ref=recv_buf.at[phase, pl.ds(dst, count)],
            send_sem=halo_s.at[phase, i],
            recv_sem=halo_r.at[phase, i],
            device_id=device,
            device_id_type=MESH,
        )

    down = (jnp.maximum(v - 1, 0), s)
    up = (jnp.minimum(v + 1, n_vol - 1), s)

    def halo_copies(phase):
        copies = []
        for d in range(1, n_sub):
            copies.append((None, halo_copy(phase, d - 1, (d - 1) * gs, s * gs, gs, sub_peer(d))))
        low, high = n_sub * gs, n_sub * gs + gv
        copies.append((v > 0, halo_copy(phase, n_sub - 1, low, high, gv, down)))
        copies.append((v < n_vol - 1, halo_copy(phase, n_sub, high, low, gv, up)))
        return copies

    def when(condition, act):
        if condition is None:
            act()
        else:
            pl.when(condition)(act)

    def send_halo(phase, before):
        sources = local_sources(trace, phase)
        copies = halo_copies(phase)
        for part in range(n_sub + 1):
            count = gs if part < n_sub - 1 else gv
            for j in range(count):
                if part < n_sub - 1:
                    peer = lax.rem(s + part + 1, n_sub)
                    codes = halo_sub[pl.ds(peer * gs + j, 1), :]
                    slot = part * gs + j
                else:
                    at = (part - n_sub + 1) * gv + j
                    codes = halo_vol[at : at + 1, :]
                    slot = n_sub * gs + at
                send_buf[phase, slot] = pick(codes, sources, 0, nothing)
            if part == 0:
                before()
            condition, copy = copies[part]
            when(condition, copy.start)

    def wait_halo(phase):
        copies = halo_copies(phase)
        for i in range(n_sub - 1):
            copies[i][1].wait_recv()
        pl.when(v < n_vol - 1)(copies[n_sub - 1][1].wait_recv)
        pl.when(v > 0)(copies[n_sub][1].wait_recv)

    def wait_sent(phase):
        for condition, copy in halo_copies(phase):
            when(condition, copy.wait_send)

    def codes_of(f, k):
        return adjacency[f : f + 1, pl.ds(pl.multiple_of(k * LANES, LANES), LANES)]

    def near_local(phase):
        sources = local_sources(trace, phase)

        def body(k, carry):
            for f in range(4):
                near[k, f * ROWS : (f + 1) * ROWS, :] = pick(codes_of(f, k), sources, 0, nothing)
            return carry

        lax.fori_loop(0, tiles, body, 0)

    def make_flux(phase):
        sources = [lambda g=g: recv_buf[phase, g] for g in range(n_remote)]

        def body(k, carry):
            one, two = carry
            for f in range(4):
                rows = slice(f * ROWS, (f + 1) * ROWS)
                nearby = pick(codes_of(f, k), sources, n_groups, near[k, rows, :])
                weight = penalty[f : f + 1, pl.ds(pl.multiple_of(k * LANES, LANES), LANES)]
                value = weight * (trace[phase, k, rows, :] - nearby)
                flux[phase, k, rows, :] = value
                if phase == 1:
                    one = one + fold_rows(value * trace[0, k, rows, :])
                    two = two + fold_rows(value * trace[1, k, rows, :])
            return one, two

        zero = jnp.zeros((8, LANES), F32)
        return lax.fori_loop(0, tiles, body, (zero, zero))

    def make_volume():
        both = lax.dot(ops[LANES:, :], field3[...], preferred_element_type=F32)
        volume[...] = jnp.where(material_one, both[FIELD:], both[:FIELD]) * stiff[...]

    def finish_image(phase, out, at):
        for k in range(tiles):
            high, low = split(flux[phase, k])
            part = lax.dot(
                back3[...],
                jnp.concatenate([high, low, high], axis=0),
                preferred_element_type=F32,
            )
            cols = slice(k * LANES, (k + 1) * LANES)
            out[at, :, cols] = volume[:, cols] + part

    def dot_tile(a, b):
        rows = fold_rows(a * b)
        total = rows[:, :LANES]
        for k in range(1, tiles):
            total = total + rows[:, k * LANES : (k + 1) * LANES]
        return total

    make_traces(0, 0)
    send_halo(0, lambda: pl.semaphore_wait(barrier, sum(count - 1 for _, count in rounds)))
    near_local(0)
    make_volume()

    cap = LANES // n_sub
    target = jnp.transpose(jnp.broadcast_to(fault_target[...], (LANES, LANES)).astype(F32))
    sent = jnp.transpose(jnp.broadcast_to(fault_send[...], (LANES, LANES)).astype(F32))
    slots = iota((LANES, LANES), 1).astype(F32)
    placed = jnp.where(target == slots, sent, -1.0)
    for t in range(n_sub):
        best = jnp.max(placed[t * cap : (t + 1) * cap], axis=0, keepdims=True)
        fault_codes[t : t + 1, :] = best.astype(jnp.int32)
    polar, azimuth = angles[0:1, :], angles[1:2, :]
    sin_polar = jnp.sin(polar)
    normal = [sin_polar * jnp.cos(azimuth), sin_polar * jnp.sin(azimuth), jnp.cos(polar)]

    wait_halo(0)
    make_flux(0)
    finish_image(0, field, 2)
    field[3] = field[2] * diag_inv[...]

    make_traces(3, 1)
    send_halo(1, lambda: None)
    near_local(1)
    make_volume()
    early = [
        dot_tile(field[1], field[0]),
        dot_tile(field[0], field[2]),
        dot_tile(field[3], field[2]),
    ]
    p_vol, q_vol = dot_tile(field[0], volume[...]), dot_tile(field[3], volume[...])

    def fault_part(phase):
        sources = local_sources(flux, phase)
        for d in range(n_sub):
            codes = fault_codes[pl.ds(lax.rem(s + d, n_sub), 1), :]
            fault_buf[d, phase] = pick(codes, sources, 0, nothing)

    fault_part(0)
    wait_halo(1)
    p_flux, q_flux = make_flux(1)

    parts = [*early, p_vol + p_flux, q_vol + q_flux]
    parts = [jnp.sum(x, axis=0, keepdims=True) for x in parts]
    tile = jnp.concatenate([*parts, jnp.zeros((3, LANES), F32)], axis=0)

    def start_sums(buf, at, peer, count):
        def body(d, carry):
            pltpu.make_async_remote_copy(
                src_ref=buf.at[0],
                dst_ref=buf.at[d],
                send_sem=sum_s.at[at],
                recv_sem=sum_r.at[at],
                device_id=peer(d),
                device_id_type=MESH,
            ).start()
            return carry

        lax.fori_loop(1, count, body, 0)

    def whole(buf, sem, at, count):
        view = buf.at[pl.ds(1, count - 1)]
        pltpu.make_async_copy(view, view, sem.at[at]).wait()

    bufs = [sums, sums_two]
    sums[0] = tile
    start_sums(sums, 0, *rounds[0])

    def fault_copy(d):
        return pltpu.make_async_remote_copy(
            src_ref=fault_buf.at[d],
            dst_ref=fault_recv.at[d - 1],
            send_sem=fault_s.at[d - 1],
            recv_sem=fault_r.at[d - 1],
            device_id=sub_peer(d),
            device_id_type=MESH,
        )

    fault_part(1)
    for d in range(1, n_sub):
        fault_copy(d).start()
    finish_image(1, image, 0)
    wait_sent(0)
    wait_sent(1)

    for at, (peer, count) in enumerate(rounds):
        whole(bufs[at], sum_r, at, count)
        total = jnp.sum(bufs[at][0:count], axis=0)
        if at + 1 < len(rounds):
            bufs[at + 1][0] = total
            start_sums(bufs[at + 1], at + 1, *rounds[at + 1])
    total = jnp.sum(total, axis=1, keepdims=True)
    rz, pw, qw, pv, qv = [total[i : i + 1] for i in range(5)]

    step = rz / pw
    rz_new = step * step * qw - rz
    ratio = rz_new / rz
    along = 1.0 + ratio
    curve = along * along * pw - along * step * (pv + qw) + step * step * qv
    step_two = rz_new / curve
    first = step + step_two * along
    second = step * step_two

    answer = first * field[0] - second * field[3]
    left_over = field[1] - first * field[2] + second * image[0]
    for c in range(3):
        solution_out[c] = answer[c * STRIDE : c * STRIDE + 20]
        residual_out[c] = left_over[c * STRIDE : c * STRIDE + 20]

    for d in range(1, n_sub):
        fault_copy(d).wait_recv()
    base, slope = fault_buf[0, 0], fault_buf[0, 1]
    for d in range(1, n_sub):
        base = base + fault_recv[d - 1, 0]
        slope = slope + fault_recv[d - 1, 1]
    grid[...] = first * base - second * slope
    vectors = [grid[c * 10 : c * 10 + 10, :] for c in range(3)]
    normal_part = vectors[0] * normal[0] + vectors[1] * normal[1] + vectors[2] * normal[2]
    shear = [vectors[c] - normal_part * normal[c] for c in range(3)]
    shear_size = jnp.sqrt(
        shear[0] * shear[0] + shear[1] * shear[1] + shear[2] * shear[2] + SHEAR_SOFT
    )
    rate, old = slip[...], sigma[...]
    fresh = old - RATE_LENGTH * (rate + SPEED_REF) * (old - (SIGMA_BACK - normal_part))
    sigma_out[...] = fresh
    slip_out[...] = jnp.maximum(rate + RATE_DAMP * (shear_size - FRICTION * fresh), 0.0)

    for d in range(1, n_sub):
        fault_copy(d).wait_send()
    for at, (peer, count) in enumerate(rounds):
        whole(bufs[at], sum_s, at, count)


def local(
    load,
    stiffness,
    material,
    stiffness_ref,
    face_trace,
    adjacency,
    penalty,
    halo_sub,
    halo_vol,
    fault_send,
    fault_target,
    fault_angles,
    slip_rate,
    sigma_eff,
):
    n_vol, n_sub = lax.axis_size("vol"), lax.axis_size("sub")
    elems = stiffness.shape[0]
    tiles = elems // LANES
    gs = halo_sub.shape[0] // n_sub // LANES
    gv = halo_vol.shape[0] // 2 // LANES
    remote = n_sub * gs + 2 * gv
    flat = n_vol * n_sub <= 64
    sizes = (n_vol, n_sub, gs, gv, tiles, flat)
    counts = (n_vol * n_sub, 1) if flat else (n_sub, n_vol)
    vmem = pl.BlockSpec(memory_space=pltpu.VMEM)
    dma = pltpu.SemaphoreType.DMA
    return pl.pallas_call(
        functools.partial(kernel, sizes),
        out_shape=(
            jax.ShapeDtypeStruct(load.shape, F32),
            jax.ShapeDtypeStruct(load.shape, F32),
            jax.ShapeDtypeStruct(slip_rate.shape, F32),
            jax.ShapeDtypeStruct(sigma_eff.shape, F32),
        ),
        in_specs=[vmem] * 14,
        out_specs=(vmem,) * 4,
        scratch_shapes=[
            pltpu.VMEM((4, FIELD, elems), F32),
            pltpu.VMEM((256, elems), BF16),
            pltpu.VMEM((LANES + 2 * FIELD, 256), BF16),
            pltpu.VMEM((FIELD, 3 * LANES), BF16),
            pltpu.VMEM((FIELD, elems), F32),
            pltpu.VMEM((2, tiles, LANES, LANES), F32),
            pltpu.VMEM((tiles, LANES, LANES), F32),
            pltpu.VMEM((2, tiles, LANES, LANES), F32),
            pltpu.VMEM((FIELD, elems), F32),
            pltpu.VMEM((1, FIELD, elems), F32),
            pltpu.VMEM((2, remote, ROWS, LANES), F32),
            pltpu.VMEM((2, remote, ROWS, LANES), F32),
            pltpu.VMEM((8, LANES), jnp.int32),
            pltpu.VMEM((n_sub, 2, ROWS, LANES), F32),
            pltpu.VMEM((max(n_sub - 1, 1), 2, ROWS, LANES), F32),
            pltpu.VMEM((counts[0], 8, LANES), F32),
            pltpu.VMEM((counts[1], 8, LANES), F32),
            pltpu.VMEM((ROWS, LANES), F32),
            dma((2, n_sub + 1)),
            dma((2, n_sub + 1)),
            dma((n_sub,)),
            dma((n_sub,)),
            dma((2,)),
            dma((2,)),
        ],
        compiler_params=pltpu.CompilerParams(
            collective_id=0, has_side_effects=True, vmem_limit_bytes=32 * 1024 * 1024
        ),
        name="cg_fault",
    )(
        load,
        stiffness.reshape(1, elems),
        material.reshape(1, elems),
        stiffness_ref,
        face_trace,
        adjacency,
        penalty,
        halo_sub.reshape(n_sub * gs, LANES),
        halo_vol.reshape(2 * gv, LANES),
        fault_send.reshape(1, LANES),
        fault_target.reshape(1, LANES),
        fault_angles,
        slip_rate,
        sigma_eff,
    )


def solution(mesh):
    return jax.shard_map(
        local,
        mesh=mesh,
        in_specs=(
            P(None, None, ("vol", "sub")),
            P(("vol", "sub")),
            P(("vol", "sub")),
            P(),
            P(),
            P(None, ("vol", "sub")),
            P(None, ("vol", "sub")),
            P(("vol", "sub")),
            P(("vol", "sub")),
            P(("vol", "sub")),
            P(("vol", "sub")),
            P(None, ("vol", "sub")),
            P(None, ("vol", "sub")),
            P(None, ("vol", "sub")),
        ),
        out_specs=(
            P(None, None, ("vol", "sub")),
            P(None, None, ("vol", "sub")),
            P(None, ("vol", "sub")),
            P(None, ("vol", "sub")),
        ),
        check_vma=False,
    )
```

```python
import functools

import jax
import jax.numpy as jnp
from jax import lax
from jax.experimental import pallas as pl
from jax.experimental.pallas import tpu as pltpu
from jax.sharding import PartitionSpec as P

FRICTION = 0.4
SIGMA_BACK = 3.0
RATE_LENGTH = 0.5
SPEED_REF = 0.2
RATE_DAMP = 0.5
SHEAR_SOFT = 0.01

HIGHEST = lax.Precision.HIGHEST
MESH = pl.DeviceIdType.MESH
F32, BF16 = jnp.float32, jnp.bfloat16
LANES = 128
ROWS = 32
STRIDE = 24
PACKED = 16
LEVELS = 32700.0
FIELD = 80


def iota(shape, dim):
    return lax.broadcasted_iota(jnp.int32, shape, dim)


def exact_dot(a, b):
    return lax.dot(a, b, precision=HIGHEST, preferred_element_type=F32)


def split(x):
    high = x.astype(BF16)
    return high, (x - high.astype(F32)).astype(BF16)


def fold_rows(x):
    total = x[0:8]
    for i in range(8, x.shape[0], 8):
        total = total + x[i : i + 8]
    return total


def pack(block):
    size = jnp.max(jnp.abs(block), axis=0, keepdims=True)
    power = jnp.ceil(jnp.log2(jnp.maximum(size, 1e-35)))
    whole = jnp.floor((block * jnp.exp2(-power)) * LEVELS + 0.5).astype(jnp.int32)
    low = whole[PACKED:]
    last = lax.broadcasted_iota(jnp.int32, low.shape, 0) == PACKED - 1
    low = jnp.where(last, jnp.broadcast_to(power.astype(jnp.int32), low.shape), low)
    return jnp.bitwise_or(lax.shift_left(whole[:PACKED], 16), jnp.bitwise_and(low, 0xFFFF))


def unpack(packed):
    high = lax.shift_right_arithmetic(packed, 16)
    low = lax.shift_right_arithmetic(lax.shift_left(packed, 16), 16)
    unit = jnp.exp2(low[PACKED - 1 : PACKED].astype(F32)) * (1.0 / LEVELS)
    last = lax.broadcasted_iota(jnp.int32, low.shape, 0) == PACKED - 1
    low = jnp.where(last, 0, low)
    return jnp.concatenate([high, low], axis=0).astype(F32) * unit


def pick(codes, sources, first, start):
    group = jnp.broadcast_to(lax.shift_right_arithmetic(codes, 7), (8, LANES))
    lane = jnp.broadcast_to(jnp.bitwise_and(codes, LANES - 1), (8, LANES))
    out = [start[8 * r : 8 * r + 8] for r in range(PACKED // 8)]
    for i, source in enumerate(sources):
        hit = group == first + i
        block = source()
        for r in range(PACKED // 8):
            taken = jnp.take_along_axis(
                block[8 * r : 8 * r + 8], lane, axis=1, mode="promise_in_bounds"
            )
            out[r] = jnp.where(hit, taken, out[r])
    return jnp.concatenate(out, axis=0)


def kernel(sizes, *refs):
    raw, outs, held, (load_sems, *rest) = refs[:14], refs[14:18], refs[18:32], refs[32:]
    loads = [pltpu.make_async_copy(a, b, load_sems.at[i]) for i, (a, b) in enumerate(zip(raw, held))]
    first = (3, 4)
    order = [*first, *(i for i in range(14) if i not in first)]
    for i in order:
        loads[i].start()

    def wait_first():
        for i in first:
            loads[i].wait()

    def wait_rest():
        for i in order[len(first) :]:
            loads[i].wait()

    run(sizes, wait_first, wait_rest, *held, *outs, *rest)


def finish(*refs):
    sems = refs[-1]
    copies = [pltpu.make_async_copy(refs[i], refs[i + 4], sems.at[i]) for i in range(4)]
    for copy in copies:
        copy.start()
    for copy in copies:
        copy.wait()


def run(
    sizes,
    wait_first,
    wait_rest,
    load,
    stiff,
    material,
    stiffness_ref,
    face_trace,
    adjacency,
    penalty,
    halo_sub,
    halo_vol,
    fault_send,
    fault_target,
    angles,
    slip,
    sigma,
    solution_out,
    residual_out,
    slip_out,
    sigma_out,
    field,
    field3,
    ops,
    back3,
    diag_inv,
    trace,
    packed,
    packed_remote,
    near,
    flux,
    volume,
    image,
    send_buf,
    recv_buf,
    fault_codes,
    fault_buf,
    fault_recv,
    sums,
    sums_two,
    grid,
    halo_s,
    halo_r,
    fault_s,
    fault_r,
    sum_s,
    sum_r,
):
    n_vol, n_sub, gs, gv, tiles, flat = sizes
    elems = tiles * LANES
    v, s = lax.axis_index("vol"), lax.axis_index("sub")
    n_groups = 4 * tiles
    n_remote = n_sub * gs + 2 * gv

    def sub_peer(d):
        return (v, lax.rem(s + d, n_sub))

    def vol_peer(d):
        return (lax.rem(v + d, n_vol), s)

    def any_peer(d):
        place = lax.rem(v * n_sub + s + d, n_vol * n_sub)
        return (lax.div(place, n_sub), lax.rem(place, n_sub))

    recv_buf[...] = jnp.zeros_like(recv_buf)
    barrier = pltpu.get_barrier_semaphore()
    rounds = [(any_peer, n_vol * n_sub)] if flat else [(sub_peer, n_sub), (vol_peer, n_vol)]
    for peer, count in rounds:

        def greet(d, carry, peer=peer):
            pl.semaphore_signal(barrier, inc=1, device_id=peer(d), device_id_type=MESH)
            return carry

        lax.fori_loop(1, count, greet, 0)

    wait_first()

    wide = 256
    col = iota((20, wide), 1)
    inner = lax.rem(col, FIELD)
    node_of = jnp.where((col < 3 * FIELD) & (inner < 3 * STRIDE), lax.rem(inner, STRIDE), -1)
    spread = (node_of == iota((20, wide), 0)).astype(F32)
    row = iota((ROWS, 10), 0)
    lift = ((lax.rem(row, 10) == iota((ROWS, 10), 1)) & (row < 30)).astype(F32)
    same = lax.div(iota((ROWS, wide), 0), 10) == lax.div(
        lax.rem(iota((ROWS, wide), 1), FIELD), STRIDE
    )
    third = iota((1, wide), 1) >= 2 * FIELD

    def store_op(at, value):
        high, low = split(value)
        ops[pl.ds(at, value.shape[0]), :] = jnp.where(
            third, low.astype(F32), high.astype(F32)
        ).astype(BF16)

    faces = []
    for f in range(4):
        full = exact_dot(exact_dot(lift, face_trace[:, f, :]), spread)
        faces.append(jnp.where(same, full, 0.0))
    face_all = jnp.concatenate(faces, axis=0)
    store_op(0, face_all)
    back = jnp.transpose(face_all[:, :LANES])[:FIELD]
    back_high, back_low = split(back)
    back3[...] = jnp.concatenate([back_high, back_high, back_low], axis=1)

    a60 = iota((60, wide), 0)
    c60 = iota((60, wide), 1)
    in60 = lax.rem(c60, FIELD)
    place60 = lax.div(in60, STRIDE) * 20 + lax.rem(in60, STRIDE)
    ok60 = (c60 < 3 * FIELD) & (in60 < 3 * STRIDE) & (lax.rem(in60, STRIDE) < 20)
    right = (ok60 & (place60 == a60)).astype(F32)
    rows60 = iota((FIELD, 60), 0)
    left = (
        (rows60 < 3 * STRIDE)
        & (lax.rem(rows60, STRIDE) < 20)
        & (lax.div(rows60, STRIDE) * 20 + lax.rem(rows60, STRIDE) == iota((FIELD, 60), 1))
    ).astype(F32)
    eye = iota((FIELD, wide), 0) == iota((FIELD, wide), 1)
    pad_row = iota((FIELD, 1), 0)
    is_pad = (pad_row >= 3 * STRIDE) | (lax.rem(pad_row, STRIDE) >= 20)
    diag = []
    for m in range(2):
        ref = exact_dot(exact_dot(left, stiffness_ref[:, m, :]), right)
        store_op(LANES + m * FIELD, ref)
        entries = jnp.sum(jnp.where(eye, ref, 0.0), axis=1, keepdims=True)
        diag.append(jnp.where(is_pad, 1.0, entries))
    squares = back * back
    weights = []
    lane_face = lax.div(iota((FIELD, LANES), 1), ROWS)
    for f in range(4):
        weights.append(jnp.sum(jnp.where(lane_face == f, squares, 0.0), axis=1, keepdims=True))

    wait_rest()

    def as_row(ref):
        return jnp.concatenate([ref[k : k + 1, :] for k in range(tiles)], axis=1)

    stiff_row = as_row(stiff)
    material_one = as_row(material) == 1
    field[...] = jnp.zeros_like(field)
    for c in range(3):
        field[1, c * STRIDE : c * STRIDE + 20, :] = load[c]
    precond = jnp.where(material_one, diag[1], diag[0]) * stiff_row
    for f in range(4):
        precond = precond + weights[f] * penalty[f : f + 1, :]
    diag_inv[...] = 1.0 / precond
    field[0] = field[1] * diag_inv[...]

    def make_traces(index, phase):
        high, low = split(field[index])
        field3[...] = jnp.concatenate(
            [high, low, high, jnp.zeros((wide - 3 * FIELD, elems), BF16)], axis=0
        )
        for k in range(tiles):
            trace[phase, k] = lax.dot(
                ops[:LANES, :],
                field3[:, k * LANES : (k + 1) * LANES],
                preferred_element_type=F32,
            )

    def pack_groups(ref, phase, at):
        for f in range(4):
            for k in range(tiles):
                packed[at, f * tiles + k] = pack(ref[phase, k, f * ROWS : (f + 1) * ROWS, :])

    def local_sources(at):
        return [lambda g=g: packed[at, g] for g in range(n_groups)]

    nothing = jnp.zeros((PACKED, LANES), jnp.int32)

    def halo_copy(phase, i, src, dst, count, device):
        return pltpu.make_async_remote_copy(
            src_ref=send_buf.at[phase, pl.ds(src, count)],
            dst_ref=recv_buf.at[phase, pl.ds(dst, count)],
            send_sem=halo_s.at[phase, i],
            recv_sem=halo_r.at[phase, i],
            device_id=device,
            device_id_type=MESH,
        )

    down = (jnp.maximum(v - 1, 0), s)
    up = (jnp.minimum(v + 1, n_vol - 1), s)

    def halo_copies(phase):
        copies = []
        for d in range(1, n_sub):
            copies.append((None, halo_copy(phase, d - 1, (d - 1) * gs, s * gs, gs, sub_peer(d))))
        low, high = n_sub * gs, n_sub * gs + gv
        copies.append((v > 0, halo_copy(phase, n_sub - 1, low, high, gv, down)))
        copies.append((v < n_vol - 1, halo_copy(phase, n_sub, high, low, gv, up)))
        return copies

    def when(condition, act):
        if condition is None:
            act()
        else:
            pl.when(condition)(act)

    def send_halo(phase, before):
        pack_groups(trace, phase, 0)
        sources = local_sources(0)
        copies = halo_copies(phase)
        for part in range(n_sub + 1):
            count = gs if part < n_sub - 1 else gv
            for j in range(count):
                if part < n_sub - 1:
                    peer = lax.rem(s + part + 1, n_sub)
                    codes = halo_sub[pl.ds(peer * gs + j, 1), :]
                    slot = part * gs + j
                else:
                    at = (part - n_sub + 1) * gv + j
                    codes = halo_vol[at : at + 1, :]
                    slot = n_sub * gs + at
                send_buf[phase, slot] = unpack(pick(codes, sources, 0, nothing))
            if part == 0:
                before()
            condition, copy = copies[part]
            when(condition, copy.start)

    def wait_halo(phase):
        copies = halo_copies(phase)
        for i in range(n_sub - 1):
            copies[i][1].wait_recv()
        pl.when(v < n_vol - 1)(copies[n_sub - 1][1].wait_recv)
        pl.when(v > 0)(copies[n_sub][1].wait_recv)

    def wait_sent(phase):
        for condition, copy in halo_copies(phase):
            when(condition, copy.wait_send)

    def codes_of(f, k):
        return adjacency[f : f + 1, k * LANES : (k + 1) * LANES]

    def near_local():
        sources = local_sources(0)
        for f in range(4):
            for k in range(tiles):
                near[f * tiles + k] = pick(codes_of(f, k), sources, 0, nothing)

    def make_flux(phase):
        for g in range(n_remote):
            packed_remote[g] = pack(recv_buf[phase, g])
        sources = [lambda g=g: packed_remote[g] for g in range(n_remote)]
        one = two = jnp.zeros((8, LANES), F32)
        for f in range(4):
            rows = slice(f * ROWS, (f + 1) * ROWS)
            for k in range(tiles):
                nearby = pick(codes_of(f, k), sources, n_groups, near[f * tiles + k])
                weight = penalty[f : f + 1, k * LANES : (k + 1) * LANES]
                value = weight * (trace[phase, k, rows, :] - unpack(nearby))
                flux[phase, k, rows, :] = value
                if phase == 1:
                    one = one + fold_rows(value * trace[0, k, rows, :])
                    two = two + fold_rows(value * trace[1, k, rows, :])
        return one, two

    def make_volume():
        both = lax.dot(ops[LANES:, :], field3[...], preferred_element_type=F32)
        volume[...] = jnp.where(material_one, both[FIELD:], both[:FIELD]) * stiff_row

    def finish_image(phase, out, at):
        for k in range(tiles):
            high, low = split(flux[phase, k])
            part = lax.dot(
                back3[...],
                jnp.concatenate([high, low, high], axis=0),
                preferred_element_type=F32,
            )
            cols = slice(k * LANES, (k + 1) * LANES)
            out[at, :, cols] = volume[:, cols] + part

    def dot_tile(a, b):
        rows = fold_rows(a * b)
        total = rows[:, :LANES]
        for k in range(1, tiles):
            total = total + rows[:, k * LANES : (k + 1) * LANES]
        return total

    make_traces(0, 0)
    send_halo(0, lambda: pl.semaphore_wait(barrier, sum(count - 1 for _, count in rounds)))
    near_local()
    make_volume()

    cap = LANES // n_sub
    target = jnp.transpose(jnp.broadcast_to(fault_target[...], (LANES, LANES)).astype(F32))
    sent = jnp.transpose(jnp.broadcast_to(fault_send[...], (LANES, LANES)).astype(F32))
    slots = iota((LANES, LANES), 1).astype(F32)
    placed = jnp.where(target == slots, sent, -1.0)
    for t in range(n_sub):
        best = jnp.max(placed[t * cap : (t + 1) * cap], axis=0, keepdims=True)
        fault_codes[t : t + 1, :] = best.astype(jnp.int32)
    polar, azimuth = angles[0:1, :], angles[1:2, :]
    sin_polar = jnp.sin(polar)
    normal = [sin_polar * jnp.cos(azimuth), sin_polar * jnp.sin(azimuth), jnp.cos(polar)]

    wait_halo(0)
    make_flux(0)
    finish_image(0, field, 2)
    field[3] = field[2] * diag_inv[...]

    make_traces(3, 1)
    send_halo(1, lambda: None)
    near_local()
    make_volume()
    early = [
        dot_tile(field[1], field[0]),
        dot_tile(field[0], field[2]),
        dot_tile(field[3], field[2]),
    ]
    p_vol, q_vol = dot_tile(field[0], volume[...]), dot_tile(field[3], volume[...])

    def fault_part(phase):
        pack_groups(flux, phase, 1)
        sources = local_sources(1)
        for d in range(n_sub):
            codes = fault_codes[pl.ds(lax.rem(s + d, n_sub), 1), :]
            fault_buf[d, phase] = unpack(pick(codes, sources, 0, nothing))

    fault_part(0)
    wait_halo(1)
    p_flux, q_flux = make_flux(1)

    parts = [*early, p_vol + p_flux, q_vol + q_flux]
    parts = [jnp.sum(x, axis=0, keepdims=True) for x in parts]
    tile = jnp.concatenate([*parts, jnp.zeros((3, LANES), F32)], axis=0)

    def start_sums(buf, at, peer, count):
        def body(d, carry):
            pltpu.make_async_remote_copy(
                src_ref=buf.at[0],
                dst_ref=buf.at[d],
                send_sem=sum_s.at[at],
                recv_sem=sum_r.at[at],
                device_id=peer(d),
                device_id_type=MESH,
            ).start()
            return carry

        lax.fori_loop(1, count, body, 0)

    def whole(buf, sem, at, count):
        view = buf.at[pl.ds(1, count - 1)]
        pltpu.make_async_copy(view, view, sem.at[at]).wait()

    bufs = [sums, sums_two]
    sums[0] = tile
    start_sums(sums, 0, *rounds[0])

    def fault_copy(d):
        return pltpu.make_async_remote_copy(
            src_ref=fault_buf.at[d],
            dst_ref=fault_recv.at[d - 1],
            send_sem=fault_s.at[d - 1],
            recv_sem=fault_r.at[d - 1],
            device_id=sub_peer(d),
            device_id_type=MESH,
        )

    fault_part(1)
    for d in range(1, n_sub):
        fault_copy(d).start()
    finish_image(1, image, 0)
    wait_sent(0)
    wait_sent(1)

    for at, (peer, count) in enumerate(rounds):
        whole(bufs[at], sum_r, at, count)
        total = jnp.sum(bufs[at][0:count], axis=0)
        if at + 1 < len(rounds):
            bufs[at + 1][0] = total
            start_sums(bufs[at + 1], at + 1, *rounds[at + 1])
    total = jnp.sum(total, axis=1, keepdims=True)
    rz, pw, qw, pv, qv = [total[i : i + 1] for i in range(5)]

    step = rz / pw
    rz_new = step * step * qw - rz
    ratio = rz_new / rz
    along = 1.0 + ratio
    curve = along * along * pw - along * step * (pv + qw) + step * step * qv
    step_two = rz_new / curve
    first = step + step_two * along
    second = step * step_two

    answer = first * field[0] - second * field[3]
    left_over = field[1] - first * field[2] + second * image[0]
    for c in range(3):
        solution_out[c] = answer[c * STRIDE : c * STRIDE + 20]
        residual_out[c] = left_over[c * STRIDE : c * STRIDE + 20]

    for d in range(1, n_sub):
        fault_copy(d).wait_recv()
    base, slope = fault_buf[0, 0], fault_buf[0, 1]
    for d in range(1, n_sub):
        base = base + fault_recv[d - 1, 0]
        slope = slope + fault_recv[d - 1, 1]
    grid[...] = first * base - second * slope
    vectors = [grid[c * 10 : c * 10 + 10, :] for c in range(3)]
    normal_part = vectors[0] * normal[0] + vectors[1] * normal[1] + vectors[2] * normal[2]
    shear = [vectors[c] - normal_part * normal[c] for c in range(3)]
    shear_size = jnp.sqrt(
        shear[0] * shear[0] + shear[1] * shear[1] + shear[2] * shear[2] + SHEAR_SOFT
    )
    rate, old = slip[...], sigma[...]
    fresh = old - RATE_LENGTH * (rate + SPEED_REF) * (old - (SIGMA_BACK - normal_part))
    sigma_out[...] = fresh
    slip_out[...] = jnp.maximum(rate + RATE_DAMP * (shear_size - FRICTION * fresh), 0.0)

    for d in range(1, n_sub):
        fault_copy(d).wait_send()
    for at, (peer, count) in enumerate(rounds):
        whole(bufs[at], sum_s, at, count)


def local(
    load,
    stiffness,
    material,
    stiffness_ref,
    face_trace,
    adjacency,
    penalty,
    halo_sub,
    halo_vol,
    fault_send,
    fault_target,
    fault_angles,
    slip_rate,
    sigma_eff,
):
    n_vol, n_sub = lax.axis_size("vol"), lax.axis_size("sub")
    elems = stiffness.shape[0]
    tiles = elems // LANES
    gs = halo_sub.shape[0] // n_sub // LANES
    gv = halo_vol.shape[0] // 2 // LANES
    remote = n_sub * gs + 2 * gv
    n_groups = 4 * tiles
    flat = n_vol * n_sub <= 64
    sizes = (n_vol, n_sub, gs, gv, tiles, flat)
    counts = (n_vol * n_sub, 1) if flat else (n_sub, n_vol)
    vmem = pl.BlockSpec(memory_space=pltpu.VMEM)
    anywhere = pl.BlockSpec(memory_space=pl.ANY)
    dma = pltpu.SemaphoreType.DMA
    inputs = (
        load,
        stiffness.reshape(tiles, LANES),
        material.reshape(tiles, LANES),
        jnp.transpose(stiffness_ref, (1, 0, 2)),
        jnp.transpose(face_trace, (1, 0, 2)),
        adjacency,
        penalty,
        halo_sub.reshape(n_sub * gs, LANES),
        halo_vol.reshape(2 * gv, LANES),
        fault_send.reshape(1, LANES),
        fault_target.reshape(1, LANES),
        fault_angles,
        slip_rate,
        sigma_eff,
    )
    shapes = tuple(jax.ShapeDtypeStruct(x.shape, F32) for x in (load, load, slip_rate, sigma_eff))
    outs = pl.pallas_call(
        functools.partial(kernel, sizes),
        out_shape=tuple(pltpu.VMEM(x.shape, x.dtype) for x in shapes),
        in_specs=[pl.BlockSpec(memory_space=pltpu.HBM)] * 14,
        out_specs=(vmem,) * 4,
        scratch_shapes=[
            *(pltpu.VMEM(x.shape, x.dtype) for x in inputs),
            dma((14,)),
            pltpu.VMEM((4, FIELD, elems), F32),
            pltpu.VMEM((256, elems), BF16),
            pltpu.VMEM((LANES + 2 * FIELD, 256), BF16),
            pltpu.VMEM((FIELD, 3 * LANES), BF16),
            pltpu.VMEM((FIELD, elems), F32),
            pltpu.VMEM((2, tiles, LANES, LANES), F32),
            pltpu.VMEM((2, n_groups, PACKED, LANES), jnp.int32),
            pltpu.VMEM((remote, PACKED, LANES), jnp.int32),
            pltpu.VMEM((n_groups, PACKED, LANES), jnp.int32),
            pltpu.VMEM((2, tiles, LANES, LANES), F32),
            pltpu.VMEM((FIELD, elems), F32),
            pltpu.VMEM((1, FIELD, elems), F32),
            pltpu.VMEM((2, remote, ROWS, LANES), F32),
            pltpu.VMEM((2, remote, ROWS, LANES), F32),
            pltpu.VMEM((8, LANES), jnp.int32),
            pltpu.VMEM((n_sub, 2, ROWS, LANES), F32),
            pltpu.VMEM((max(n_sub - 1, 1), 2, ROWS, LANES), F32),
            pltpu.VMEM((counts[0], 8, LANES), F32),
            pltpu.VMEM((counts[1], 8, LANES), F32),
            pltpu.VMEM((ROWS, LANES), F32),
            dma((2, n_sub + 1)),
            dma((2, n_sub + 1)),
            dma((n_sub,)),
            dma((n_sub,)),
            dma((2,)),
            dma((2,)),
        ],
        compiler_params=pltpu.CompilerParams(collective_id=0, has_side_effects=True, vmem_limit_bytes=32 * 1024 * 1024),
        name="cg_fault",
    )(*(pltpu.with_memory_space_constraint(x, pltpu.HBM) for x in inputs))
    return pl.pallas_call(
        finish,
        out_shape=shapes,
        in_specs=[vmem] * 4,
        out_specs=(anywhere,) * 4,
        scratch_shapes=[dma((4,))],
        compiler_params=pltpu.CompilerParams(vmem_limit_bytes=16 * 1024 * 1024),
        name="finish",
    )(*(pltpu.with_memory_space_constraint(x, pltpu.VMEM) for x in outs))


def solution(mesh):
    return jax.shard_map(
        local,
        mesh=mesh,
        in_specs=(
            P(None, None, ("vol", "sub")),
            P(("vol", "sub")),
            P(("vol", "sub")),
            P(),
            P(),
            P(None, ("vol", "sub")),
            P(None, ("vol", "sub")),
            P(("vol", "sub")),
            P(("vol", "sub")),
            P(("vol", "sub")),
            P(("vol", "sub")),
            P(None, ("vol", "sub")),
            P(None, ("vol", "sub")),
            P(None, ("vol", "sub")),
        ),
        out_specs=(
            P(None, None, ("vol", "sub")),
            P(None, None, ("vol", "sub")),
            P(None, ("vol", "sub")),
            P(None, ("vol", "sub")),
        ),
        check_vma=False,
    )
```

```python
import functools

import jax
import jax.numpy as jnp
from jax import lax
from jax.experimental import pallas as pl
from jax.experimental.pallas import tpu as pltpu
from jax.sharding import PartitionSpec as P

FRICTION = 0.4
SIGMA_BACK = 3.0
RATE_LENGTH = 0.5
SPEED_REF = 0.2
RATE_DAMP = 0.5
SHEAR_SOFT = 0.01

MESH = pl.DeviceIdType.MESH
F32, BF16 = jnp.float32, jnp.bfloat16
LANES = 128
ROWS = 32
STRIDE = 24
PACKED = 16
LEVELS = 32700.0
FIELD = 80


def iota(shape, dim):
    return lax.broadcasted_iota(jnp.int32, shape, dim)


def place(rows, value, cols):
    moved = lax.dot(rows, value, preferred_element_type=F32).astype(BF16)
    return lax.dot(moved, cols, preferred_element_type=F32)


def split(x):
    high = x.astype(BF16)
    return high, (x - high.astype(F32)).astype(BF16)


def fold_rows(x):
    total = x[0:8]
    for i in range(8, x.shape[0], 8):
        total = total + x[i : i + 8]
    return total


def pack(block):
    size = jnp.max(jnp.abs(block), axis=0, keepdims=True)
    power = jnp.ceil(jnp.log2(jnp.maximum(size, 1e-35)))
    whole = jnp.floor((block * jnp.exp2(-power)) * LEVELS + 0.5).astype(jnp.int32)
    low = whole[PACKED:]
    last = lax.broadcasted_iota(jnp.int32, low.shape, 0) == PACKED - 1
    low = jnp.where(last, jnp.broadcast_to(power.astype(jnp.int32), low.shape), low)
    return jnp.bitwise_or(lax.shift_left(whole[:PACKED], 16), jnp.bitwise_and(low, 0xFFFF))


def unpack(packed):
    high = lax.shift_right_arithmetic(packed, 16)
    low = lax.shift_right_arithmetic(lax.shift_left(packed, 16), 16)
    unit = jnp.exp2(low[PACKED - 1 : PACKED].astype(F32)) * (1.0 / LEVELS)
    last = lax.broadcasted_iota(jnp.int32, low.shape, 0) == PACKED - 1
    low = jnp.where(last, 0, low)
    return jnp.concatenate([high, low], axis=0).astype(F32) * unit


def pick(codes, sources, first, start):
    group = jnp.broadcast_to(lax.shift_right_arithmetic(codes, 7), (8, LANES))
    lane = jnp.broadcast_to(jnp.bitwise_and(codes, LANES - 1), (8, LANES))
    out = [start[8 * r : 8 * r + 8] for r in range(PACKED // 8)]
    for i, source in enumerate(sources):
        hit = group == first + i
        block = source()
        for r in range(PACKED // 8):
            taken = jnp.take_along_axis(
                block[8 * r : 8 * r + 8], lane, axis=1, mode="promise_in_bounds"
            )
            out[r] = jnp.where(hit, taken, out[r])
    return jnp.concatenate(out, axis=0)


def kernel(sizes, *refs):
    raw, outs, held, (load_sems, *rest) = refs[:14], refs[14:18], refs[18:32], refs[32:]
    loads = [pltpu.make_async_copy(a, b, load_sems.at[i]) for i, (a, b) in enumerate(zip(raw, held))]
    first = (3, 4)
    order = [*first, *(i for i in range(14) if i not in first)]
    for i in order:
        loads[i].start()

    def wait_first():
        for i in first:
            loads[i].wait()

    def wait_rest():
        for i in order[len(first) :]:
            loads[i].wait()

    run(sizes, wait_first, wait_rest, *held, *outs, *rest)


def finish(*refs):
    sems = refs[-1]
    copies = [pltpu.make_async_copy(refs[i], refs[i + 4], sems.at[i]) for i in range(4)]
    for copy in copies:
        copy.start()
    for copy in copies:
        copy.wait()


def run(
    sizes,
    wait_first,
    wait_rest,
    load,
    stiff,
    material,
    stiffness_ref,
    face_trace,
    adjacency,
    penalty,
    halo_sub,
    halo_vol,
    fault_send,
    fault_target,
    angles,
    slip,
    sigma,
    solution_out,
    residual_out,
    slip_out,
    sigma_out,
    field,
    field3,
    ops,
    back3,
    diag_inv,
    trace,
    packed,
    packed_remote,
    near,
    flux,
    volume,
    image,
    send_buf,
    recv_buf,
    fault_codes,
    fault_buf,
    fault_recv,
    sums,
    sums_two,
    grid,
    halo_s,
    halo_r,
    fault_s,
    fault_r,
    sum_s,
    sum_r,
):
    n_vol, n_sub, gs, gv, tiles, flat = sizes
    elems = tiles * LANES
    v, s = lax.axis_index("vol"), lax.axis_index("sub")
    n_groups = 4 * tiles
    n_remote = n_sub * gs + 2 * gv

    def sub_peer(d):
        return (v, lax.rem(s + d, n_sub))

    def vol_peer(d):
        return (lax.rem(v + d, n_vol), s)

    def any_peer(d):
        place = lax.rem(v * n_sub + s + d, n_vol * n_sub)
        return (lax.div(place, n_sub), lax.rem(place, n_sub))

    recv_buf[...] = jnp.zeros_like(recv_buf)
    barrier = pltpu.get_barrier_semaphore()
    rounds = [(any_peer, n_vol * n_sub)] if flat else [(sub_peer, n_sub), (vol_peer, n_vol)]
    for peer, count in rounds:

        def greet(d, carry, peer=peer):
            pl.semaphore_signal(barrier, inc=1, device_id=peer(d), device_id_type=MESH)
            return carry

        lax.fori_loop(1, count, greet, 0, unroll=flat)

    wait_first()

    wide = 256
    col = iota((20, wide), 1)
    inner = lax.rem(col, FIELD)
    node_of = jnp.where((col < 3 * FIELD) & (inner < 3 * STRIDE), lax.rem(inner, STRIDE), -1)
    spread = (node_of == iota((20, wide), 0)).astype(F32).astype(BF16)
    row = iota((ROWS, 10), 0)
    lift = ((lax.rem(row, 10) == iota((ROWS, 10), 1)) & (row < 30)).astype(F32).astype(BF16)
    same = lax.div(iota((ROWS, wide), 0), 10) == lax.div(
        lax.rem(iota((ROWS, wide), 1), FIELD), STRIDE
    )
    third = iota((1, wide), 1) >= 2 * FIELD

    def store_op(at, high, low):
        ops[pl.ds(at, high.shape[0]), :] = jnp.where(third, low, high).astype(BF16)

    faces = []
    for f in range(4):
        parts = split(face_trace[:, f, :])
        faces.append([jnp.where(same, place(lift, part, spread), 0.0) for part in parts])
    face_high, face_low = [jnp.concatenate([face[i] for face in faces], axis=0) for i in range(2)]
    store_op(0, face_high, face_low)
    back_high, back_low = [jnp.transpose(x[:, :LANES])[:FIELD] for x in (face_high, face_low)]
    back = back_high + back_low
    back_high, back_low = back_high.astype(BF16), back_low.astype(BF16)
    back3[...] = jnp.concatenate([back_high, back_high, back_low], axis=1)

    a60 = iota((60, wide), 0)
    c60 = iota((60, wide), 1)
    in60 = lax.rem(c60, FIELD)
    place60 = lax.div(in60, STRIDE) * 20 + lax.rem(in60, STRIDE)
    ok60 = (c60 < 3 * FIELD) & (in60 < 3 * STRIDE) & (lax.rem(in60, STRIDE) < 20)
    right = (ok60 & (place60 == a60)).astype(F32).astype(BF16)
    rows60 = iota((FIELD, 60), 0)
    left = (
        (rows60 < 3 * STRIDE)
        & (lax.rem(rows60, STRIDE) < 20)
        & (lax.div(rows60, STRIDE) * 20 + lax.rem(rows60, STRIDE) == iota((FIELD, 60), 1))
    ).astype(F32).astype(BF16)
    eye = iota((FIELD, wide), 0) == iota((FIELD, wide), 1)
    pad_row = iota((FIELD, 1), 0)
    is_pad = (pad_row >= 3 * STRIDE) | (lax.rem(pad_row, STRIDE) >= 20)
    diag = []
    for m in range(2):
        high, low = [place(left, part, right) for part in split(stiffness_ref[:, m, :])]
        store_op(LANES + m * FIELD, high, low)
        entries = jnp.sum(jnp.where(eye, high + low, 0.0), axis=1, keepdims=True)
        diag.append(jnp.where(is_pad, 1.0, entries))
    squares = back * back
    weights = []
    lane_face = lax.div(iota((FIELD, LANES), 1), ROWS)
    for f in range(4):
        weights.append(jnp.sum(jnp.where(lane_face == f, squares, 0.0), axis=1, keepdims=True))

    wait_rest()

    def as_row(ref):
        return jnp.concatenate([ref[k : k + 1, :] for k in range(tiles)], axis=1)

    stiff_row = as_row(stiff)
    material_one = as_row(material) == 1
    field[...] = jnp.zeros_like(field)
    for c in range(3):
        field[1, c * STRIDE : c * STRIDE + 20, :] = load[c]
    precond = jnp.where(material_one, diag[1], diag[0]) * stiff_row
    for f in range(4):
        precond = precond + weights[f] * penalty[f : f + 1, :]
    diag_inv[...] = 1.0 / precond
    field[0] = field[1] * diag_inv[...]

    def make_traces(index, phase):
        high, low = split(field[index])
        field3[...] = jnp.concatenate(
            [high, low, high, jnp.zeros((wide - 3 * FIELD, elems), BF16)], axis=0
        )
        for k in range(tiles):
            trace[phase, k] = lax.dot(
                ops[:LANES, :],
                field3[:, k * LANES : (k + 1) * LANES],
                preferred_element_type=F32,
            )

    def pack_traces(phase):
        for f in range(4):
            for k in range(tiles):
                packed[f * tiles + k] = pack(trace[phase, k, f * ROWS : (f + 1) * ROWS, :])

    def local_sources():
        return [lambda g=g: packed[g] for g in range(n_groups)]

    nothing = jnp.zeros((PACKED, LANES), jnp.int32)

    def halo_copy(phase, i, src, dst, count, device):
        return pltpu.make_async_remote_copy(
            src_ref=send_buf.at[phase, pl.ds(src, count)],
            dst_ref=recv_buf.at[phase, pl.ds(dst, count)],
            send_sem=halo_s.at[phase, i],
            recv_sem=halo_r.at[phase, i],
            device_id=device,
            device_id_type=MESH,
        )

    down = (jnp.maximum(v - 1, 0), s)
    up = (jnp.minimum(v + 1, n_vol - 1), s)

    def halo_copies(phase):
        copies = []
        for d in range(1, n_sub):
            copies.append((None, halo_copy(phase, d - 1, (d - 1) * gs, s * gs, gs, sub_peer(d))))
        low, high = n_sub * gs, n_sub * gs + gv
        copies.append((v > 0, halo_copy(phase, n_sub - 1, low, high, gv, down)))
        copies.append((v < n_vol - 1, halo_copy(phase, n_sub, high, low, gv, up)))
        return copies

    def when(condition, act):
        if condition is None:
            act()
        else:
            pl.when(condition)(act)

    def send_halo(phase, before):
        pack_traces(phase)
        sources = local_sources()
        copies = halo_copies(phase)
        for part in range(n_sub + 1):
            count = gs if part < n_sub - 1 else gv
            for j in range(count):
                if part < n_sub - 1:
                    peer = lax.rem(s + part + 1, n_sub)
                    codes = halo_sub[pl.ds(peer * gs + j, 1), :]
                    slot = part * gs + j
                else:
                    at = (part - n_sub + 1) * gv + j
                    codes = halo_vol[at : at + 1, :]
                    slot = n_sub * gs + at
                send_buf[phase, slot] = unpack(pick(codes, sources, 0, nothing))
            if part == 0:
                before()
            condition, copy = copies[part]
            when(condition, copy.start)

    def wait_halo(phase):
        copies = halo_copies(phase)
        for i in range(n_sub - 1):
            copies[i][1].wait_recv()
        pl.when(v < n_vol - 1)(copies[n_sub - 1][1].wait_recv)
        pl.when(v > 0)(copies[n_sub][1].wait_recv)

    def wait_sent(phase):
        for condition, copy in halo_copies(phase):
            when(condition, copy.wait_send)

    def codes_of(f, k):
        return adjacency[f : f + 1, k * LANES : (k + 1) * LANES]

    def near_local():
        sources = local_sources()
        for f in range(4):
            for k in range(tiles):
                near[f * tiles + k] = pick(codes_of(f, k), sources, 0, nothing)

    def make_flux(phase):
        for g in range(n_remote):
            packed_remote[g] = pack(recv_buf[phase, g])
        sources = [lambda g=g: packed_remote[g] for g in range(n_remote)]
        one = two = jnp.zeros((8, LANES), F32)
        for f in range(4):
            rows = slice(f * ROWS, (f + 1) * ROWS)
            for k in range(tiles):
                nearby = pick(codes_of(f, k), sources, n_groups, near[f * tiles + k])
                weight = penalty[f : f + 1, k * LANES : (k + 1) * LANES]
                value = weight * (trace[phase, k, rows, :] - unpack(nearby))
                flux[phase, k, rows, :] = value
                if phase == 1:
                    one = one + fold_rows(value * trace[0, k, rows, :])
                    two = two + fold_rows(value * trace[1, k, rows, :])
        return one, two

    def make_volume():
        both = lax.dot(ops[LANES:, :], field3[...], preferred_element_type=F32)
        volume[...] = jnp.where(material_one, both[FIELD:], both[:FIELD]) * stiff_row

    def finish_image(phase, out, at):
        for k in range(tiles):
            high, low = split(flux[phase, k])
            part = lax.dot(
                back3[...],
                jnp.concatenate([high, low, high], axis=0),
                preferred_element_type=F32,
            )
            cols = slice(k * LANES, (k + 1) * LANES)
            out[at, :, cols] = volume[:, cols] + part

    def dot_tile(a, b):
        rows = fold_rows(a * b)
        total = rows[:, :LANES]
        for k in range(1, tiles):
            total = total + rows[:, k * LANES : (k + 1) * LANES]
        return total

    def pick_weight(codes):
        group = jnp.broadcast_to(lax.shift_right_arithmetic(codes, 7), (8, LANES))
        lane = jnp.broadcast_to(jnp.bitwise_and(codes, LANES - 1), (8, LANES))
        out = jnp.zeros((8, LANES), F32)
        for g in range(n_groups):
            f, k = g // tiles, g % tiles
            block = jnp.broadcast_to(penalty[f : f + 1, k * LANES : (k + 1) * LANES], (8, LANES))
            taken = jnp.take_along_axis(block, lane, axis=1, mode="promise_in_bounds")
            out = jnp.where(group == g, taken, out)
        return out[0:1]

    def fault_part(phase):
        own = local_sources()
        others = [lambda g=g: near[g] for g in range(n_groups)]
        for d in range(n_sub):
            codes = fault_codes[pl.ds(lax.rem(s + d, n_sub), 1), :]
            jump = unpack(pick(codes, own, 0, nothing)) - unpack(pick(codes, others, 0, nothing))
            fault_buf[d, phase] = pick_weight(codes) * jump

    def fault_copy(d):
        return pltpu.make_async_remote_copy(
            src_ref=fault_buf.at[d],
            dst_ref=fault_recv.at[d - 1],
            send_sem=fault_s.at[d - 1],
            recv_sem=fault_r.at[d - 1],
            device_id=sub_peer(d),
            device_id_type=MESH,
        )

    make_traces(0, 0)
    send_halo(0, lambda: pl.semaphore_wait(barrier, sum(count - 1 for _, count in rounds)))
    near_local()
    make_volume()

    cap = LANES // n_sub
    target = jnp.transpose(jnp.broadcast_to(fault_target[...], (LANES, LANES)).astype(F32))
    sent = jnp.transpose(jnp.broadcast_to(fault_send[...], (LANES, LANES)).astype(F32))
    slots = iota((LANES, LANES), 1).astype(F32)
    placed = jnp.where(target == slots, sent, -1.0)
    for t in range(n_sub):
        best = jnp.max(placed[t * cap : (t + 1) * cap], axis=0, keepdims=True)
        fault_codes[t : t + 1, :] = best.astype(jnp.int32)
    polar, azimuth = angles[0:1, :], angles[1:2, :]
    sin_polar = jnp.sin(polar)
    normal = [sin_polar * jnp.cos(azimuth), sin_polar * jnp.sin(azimuth), jnp.cos(polar)]

    fault_part(0)
    wait_halo(0)
    make_flux(0)
    finish_image(0, field, 2)
    field[3] = field[2] * diag_inv[...]

    make_traces(3, 1)
    send_halo(1, lambda: None)
    near_local()
    make_volume()
    early = [
        dot_tile(field[1], field[0]),
        dot_tile(field[0], field[2]),
        dot_tile(field[3], field[2]),
    ]
    p_vol, q_vol = dot_tile(field[0], volume[...]), dot_tile(field[3], volume[...])

    fault_part(1)
    for d in range(1, n_sub):
        fault_copy(d).start()
    wait_halo(1)
    p_flux, q_flux = make_flux(1)

    parts = [*early, p_vol + p_flux, q_vol + q_flux]
    parts = [jnp.sum(x, axis=0, keepdims=True) for x in parts]
    tile = jnp.concatenate([*parts, jnp.zeros((3, LANES), F32)], axis=0)
    tile = jnp.broadcast_to(jnp.sum(tile, axis=1, keepdims=True), (8, LANES))
    on_lane = iota((8, LANES), 0) == iota((8, LANES), 1)
    line = jnp.sum(jnp.where(on_lane, tile, 0.0), axis=0, keepdims=True)

    def start_sums(buf, at, peer, count):
        def body(d, carry):
            pltpu.make_async_remote_copy(
                src_ref=buf.at[0],
                dst_ref=buf.at[d],
                send_sem=sum_s.at[at],
                recv_sem=sum_r.at[at],
                device_id=peer(d),
                device_id_type=MESH,
            ).start()
            return carry

        lax.fori_loop(1, count, body, 0, unroll=flat)

    def whole(buf, sem, at, count):
        view = buf.at[pl.ds(1, count - 1)]
        pltpu.make_async_copy(view, view, sem.at[at]).wait()

    bufs = [sums, sums_two]
    sums[0] = line
    start_sums(sums, 0, *rounds[0])

    finish_image(1, image, 0)
    wait_sent(0)
    wait_sent(1)

    for at, (peer, count) in enumerate(rounds):
        whole(bufs[at], sum_r, at, count)
        total = jnp.sum(bufs[at][0:count], axis=0)
        if at + 1 < len(rounds):
            bufs[at + 1][0] = total
            start_sums(bufs[at + 1], at + 1, *rounds[at + 1])
    rz, pw, qw, pv, qv = [total[:, i : i + 1] for i in range(5)]

    step = rz / pw
    rz_new = step * step * qw - rz
    ratio = rz_new / rz
    along = 1.0 + ratio
    curve = along * along * pw - along * step * (pv + qw) + step * step * qv
    step_two = rz_new / curve
    first = step + step_two * along
    second = step * step_two

    answer = first * field[0] - second * field[3]
    left_over = field[1] - first * field[2] + second * image[0]
    for c in range(3):
        solution_out[c] = answer[c * STRIDE : c * STRIDE + 20]
        residual_out[c] = left_over[c * STRIDE : c * STRIDE + 20]

    for d in range(1, n_sub):
        fault_copy(d).wait_recv()
    base, slope = fault_buf[0, 0], fault_buf[0, 1]
    for d in range(1, n_sub):
        base = base + fault_recv[d - 1, 0]
        slope = slope + fault_recv[d - 1, 1]
    grid[...] = first * base - second * slope
    vectors = [grid[c * 10 : c * 10 + 10, :] for c in range(3)]
    normal_part = vectors[0] * normal[0] + vectors[1] * normal[1] + vectors[2] * normal[2]
    shear = [vectors[c] - normal_part * normal[c] for c in range(3)]
    shear_size = jnp.sqrt(
        shear[0] * shear[0] + shear[1] * shear[1] + shear[2] * shear[2] + SHEAR_SOFT
    )
    rate, old = slip[...], sigma[...]
    fresh = old - RATE_LENGTH * (rate + SPEED_REF) * (old - (SIGMA_BACK - normal_part))
    sigma_out[...] = fresh
    slip_out[...] = jnp.maximum(rate + RATE_DAMP * (shear_size - FRICTION * fresh), 0.0)

    for d in range(1, n_sub):
        fault_copy(d).wait_send()
    for at, (peer, count) in enumerate(rounds):
        whole(bufs[at], sum_s, at, count)


def local(
    load,
    stiffness,
    material,
    stiffness_ref,
    face_trace,
    adjacency,
    penalty,
    halo_sub,
    halo_vol,
    fault_send,
    fault_target,
    fault_angles,
    slip_rate,
    sigma_eff,
):
    n_vol, n_sub = lax.axis_size("vol"), lax.axis_size("sub")
    elems = stiffness.shape[0]
    tiles = elems // LANES
    gs = halo_sub.shape[0] // n_sub // LANES
    gv = halo_vol.shape[0] // 2 // LANES
    remote = n_sub * gs + 2 * gv
    n_groups = 4 * tiles
    flat = n_vol * n_sub <= 64
    sizes = (n_vol, n_sub, gs, gv, tiles, flat)
    counts = (n_vol * n_sub, 1) if flat else (n_sub, n_vol)
    vmem = pl.BlockSpec(memory_space=pltpu.VMEM)
    anywhere = pl.BlockSpec(memory_space=pl.ANY)
    dma = pltpu.SemaphoreType.DMA
    inputs = (
        load,
        stiffness.reshape(tiles, LANES),
        material.reshape(tiles, LANES),
        jnp.transpose(stiffness_ref, (1, 0, 2)),
        jnp.transpose(face_trace, (1, 0, 2)),
        adjacency,
        penalty,
        halo_sub.reshape(n_sub * gs, LANES),
        halo_vol.reshape(2 * gv, LANES),
        fault_send.reshape(1, LANES),
        fault_target.reshape(1, LANES),
        fault_angles,
        slip_rate,
        sigma_eff,
    )
    shapes = tuple(jax.ShapeDtypeStruct(x.shape, F32) for x in (load, load, slip_rate, sigma_eff))
    outs = pl.pallas_call(
        functools.partial(kernel, sizes),
        out_shape=tuple(pltpu.VMEM(x.shape, x.dtype) for x in shapes),
        in_specs=[pl.BlockSpec(memory_space=pltpu.HBM)] * 14,
        out_specs=(vmem,) * 4,
        scratch_shapes=[
            *(pltpu.VMEM(x.shape, x.dtype) for x in inputs),
            dma((14,)),
            pltpu.VMEM((4, FIELD, elems), F32),
            pltpu.VMEM((256, elems), BF16),
            pltpu.VMEM((LANES + 2 * FIELD, 256), BF16),
            pltpu.VMEM((FIELD, 3 * LANES), BF16),
            pltpu.VMEM((FIELD, elems), F32),
            pltpu.VMEM((2, tiles, LANES, LANES), F32),
            pltpu.VMEM((n_groups, PACKED, LANES), jnp.int32),
            pltpu.VMEM((remote, PACKED, LANES), jnp.int32),
            pltpu.VMEM((n_groups, PACKED, LANES), jnp.int32),
            pltpu.VMEM((2, tiles, LANES, LANES), F32),
            pltpu.VMEM((FIELD, elems), F32),
            pltpu.VMEM((1, FIELD, elems), F32),
            pltpu.VMEM((2, remote, ROWS, LANES), F32),
            pltpu.VMEM((2, remote, ROWS, LANES), F32),
            pltpu.VMEM((8, LANES), jnp.int32),
            pltpu.VMEM((n_sub, 2, ROWS, LANES), F32),
            pltpu.VMEM((max(n_sub - 1, 1), 2, ROWS, LANES), F32),
            pltpu.VMEM((counts[0], 1, LANES), F32),
            pltpu.VMEM((counts[1], 1, LANES), F32),
            pltpu.VMEM((ROWS, LANES), F32),
            dma((2, n_sub + 1)),
            dma((2, n_sub + 1)),
            dma((n_sub,)),
            dma((n_sub,)),
            dma((2,)),
            dma((2,)),
        ],
        compiler_params=pltpu.CompilerParams(collective_id=0, has_side_effects=True, vmem_limit_bytes=32 * 1024 * 1024),
        name="cg_fault",
    )(*(pltpu.with_memory_space_constraint(x, pltpu.HBM) for x in inputs))
    return pl.pallas_call(
        finish,
        out_shape=shapes,
        in_specs=[vmem] * 4,
        out_specs=(anywhere,) * 4,
        scratch_shapes=[dma((4,))],
        compiler_params=pltpu.CompilerParams(vmem_limit_bytes=16 * 1024 * 1024),
        name="finish",
    )(*(pltpu.with_memory_space_constraint(x, pltpu.VMEM) for x in outs))


def solution(mesh):
    return jax.shard_map(
        local,
        mesh=mesh,
        in_specs=(
            P(None, None, ("vol", "sub")),
            P(("vol", "sub")),
            P(("vol", "sub")),
            P(),
            P(),
            P(None, ("vol", "sub")),
            P(None, ("vol", "sub")),
            P(("vol", "sub")),
            P(("vol", "sub")),
            P(("vol", "sub")),
            P(("vol", "sub")),
            P(None, ("vol", "sub")),
            P(None, ("vol", "sub")),
            P(None, ("vol", "sub")),
        ),
        out_specs=(
            P(None, None, ("vol", "sub")),
            P(None, None, ("vol", "sub")),
            P(None, ("vol", "sub")),
            P(None, ("vol", "sub")),
        ),
        check_vma=False,
    )
```
